32 devices in a mesh: grp: 4 (over x, core), pair: 8 (over z, y).
Axes of the slice: x: 2, y: 2, z: 4, core: 2. Of those that a mesh axis runs over, the one named last changes fastest.
Arguments:
- chol: bfloat16 [128, 1024, 1024], P(None, 'pair'), may hold values from -0.1875 to 0.1875
- trial: bfloat16 [1024, 512], replicated, may hold values from -2 to 2
- walkers: float32 [32, 1024, 512], P(('grp', 'pair')), may hold values from -10 to 10
- fields: float32 [32, 128], P('grp'), may hold values from -6 to 6
- weights: float32 [32], P(('grp', 'pair')), may hold values from 0.5 to 5
Outputs:
- new_walkers: float32 [32, 1024, 512], P(('grp', 'pair'))
- half_green: float32 [32, 1024, 512], P(('grp', 'pair'))
- new_weights: float32 [32], P(('grp', 'pair'))
The draws below stay inside these ranges and needn't reach their ends.
All inputs are finite; a program needn't handle non-finite values.
Results may differ from the reference program's by a relative error of at most 0.012.
The reference program's roundings to bfloat16 on the way (of `theta`, `green`, `shifted` and `operator`) count: a program that leaves them out, or rounds other values in their place, can miss the bound.
Values may be sent and summed in bfloat16 or wider, within the bound.
A program may use at most 128 MiB of HBM per device.

```python
import jax
import jax.numpy as jnp
from jax import lax

M = 1024
N = 512
CHOL = 128
TAYLOR = 4
NS_ITERS = 3
WALKERS = 32


def draw_trial(key, part):
    first, second = jax.random.split(jax.random.fold_in(key, 11))
    top = jnp.eye(N, dtype=jnp.float32) + 0.15 * jnp.clip(jax.random.normal(first, (N, N), jnp.float32), -4.0, 4.0) / jnp.sqrt(float(N))
    bottom = 0.5 * jnp.clip(jax.random.normal(second, (M - N, N), jnp.float32), -4.0, 4.0) / jnp.sqrt(float(N))
    return jnp.concatenate([top, bottom], axis=0).astype(jnp.bfloat16)


def draw_walkers(key, part):
    first, second, third = jax.random.split(jax.random.fold_in(key, 23), 3)
    spread = 0.15
    scales = jnp.exp(jax.random.uniform(third, (WALKERS, 1, N), jnp.float32, 0.0, jnp.log(2.0)))
    top = jnp.eye(N, dtype=jnp.float32)[None] + spread * jnp.clip(jax.random.normal(first, (WALKERS, N, N), jnp.float32), -4.0, 4.0) / jnp.sqrt(float(N))
    bottom = 0.5 * jnp.clip(jax.random.normal(second, (WALKERS, M - N, N), jnp.float32), -4.0, 4.0) / jnp.sqrt(float(N))
    return jnp.concatenate([top, bottom], axis=1) * scales


def draw_weights(key, part):
    first = jax.random.fold_in(key, 37)
    steps = jnp.arange(WALKERS, dtype=jnp.float32) / max(WALKERS - 1, 1)
    base = jnp.exp(jnp.log(3.0) * steps)
    factor = jax.random.uniform(first, (WALKERS,), jnp.float32, 0.8, 1.25)
    return base * factor


def block_levels(rng, dims, shards, least, high):
    def one(position, blocks):
        steps = jax.random.uniform(jax.random.fold_in(jax.random.fold_in(rng, 6), position), (blocks,), jnp.float32, least / len(shards), high / len(shards))
        return jnp.repeat(jnp.exp(steps), dims[position] // blocks).reshape((-1,) + (1,) * (len(dims) - position - 1))

    loudness = one(*shards[0])
    for cut in shards[1:]:
        loudness = loudness * one(*cut)
    return loudness


def centred(rng, shape, width, most, cuts=(), kind=jnp.bfloat16):
    loudness = block_levels(rng, shape, cuts, -0.22, 0.18) if cuts else 1.0
    drawn = jax.random.normal(rng, shape, jnp.float32) * width * loudness
    return jnp.minimum(jnp.maximum(drawn, -most), most).astype(kind)


def setup_inputs(seed: int = 0) -> dict:
    keys = jax.random.split(jax.random.key(seed), 6)
    chol = centred(keys[0], (CHOL, M, M), (M * CHOL // 128) ** -0.5, 0.1875, ((1, 8),))
    trial = draw_trial(jax.random.fold_in(keys[5], 71), 0)
    walkers = draw_walkers(jax.random.fold_in(keys[5], 71), 0)
    fields = centred(keys[3], (WALKERS, CHOL), 1.0, 6.0, ((0, 4),), jnp.float32)
    weights = draw_weights(jax.random.fold_in(keys[5], 71), 0)
    return {"chol": chol, "trial": trial, "walkers": walkers, "fields": fields, "weights": weights}


root_step = 0.07


def newton(inner):
    entries = jnp.diagonal(inner)
    inverse = jnp.eye(N, dtype=jnp.float32) / entries[None, :]
    for sweep in range(NS_ITERS):
        product = jnp.dot(inner, inverse, precision=lax.Precision.HIGHEST)
        inverse = 2.0 * inverse - jnp.dot(inverse, product, precision=lax.Precision.HIGHEST)
    return inverse


def reference(chol, trial, walkers, fields, weights):
    trial_wide = trial.astype(jnp.float32)
    chol_flat = chol.reshape(CHOL, M * M)

    def one_walker(items):
        orbitals, draws, weight = items
        inner = jnp.dot(trial_wide.T, orbitals, precision=lax.Precision.HIGHEST)
        inverse = newton(inner)
        theta = jnp.dot(orbitals, inverse, precision=lax.Precision.HIGHEST).astype(jnp.bfloat16)
        green = jnp.dot(theta, trial.T, preferred_element_type=jnp.float32).astype(jnp.bfloat16)
        bias = jnp.dot(chol_flat, green.reshape(M * M), preferred_element_type=jnp.float32)
        xbar = -root_step * bias
        shifted = (draws - xbar).astype(jnp.bfloat16)
        operator = (root_step * jnp.dot(shifted, chol_flat, preferred_element_type=jnp.float32)).reshape(M, M).astype(jnp.bfloat16)
        term = orbitals
        total = orbitals
        for order in range(1, TAYLOR + 1):
            term = jnp.dot(operator, term.astype(jnp.bfloat16), preferred_element_type=jnp.float32) / float(order)
            total = total + term
        inner_next = jnp.dot(trial_wide.T, total, precision=lax.Precision.HIGHEST)
        inverse_next = newton(inner_next)
        half = jnp.dot(total, inverse_next, precision=lax.Precision.HIGHEST)
        raw = weight * jnp.exp(jnp.sum(draws * xbar - 0.5 * xbar * xbar))
        return total, half, raw

    new_walkers, half_green, raw = lax.map(one_walker, (walkers, fields, weights))
    new_weights = raw * (WALKERS / jnp.sum(raw))
    return new_walkers, half_green, new_weights
```

```python
import functools

import jax
import jax.numpy as jnp
from jax import lax
from jax.experimental import pallas as pl
from jax.experimental.pallas import tpu as pltpu
from jax.sharding import PartitionSpec as P

TAYLOR = 4
NS_ITERS = 3

root_step = 0.07

NT = (((1,), (1,)), ((), ()))
MESH = pl.DeviceIdType.MESH


def product(left, right):
    return jnp.dot(left, right, precision=lax.Precision.HIGH)


def newton(inner):
    size = inner.shape[-1]
    diagonal = jnp.eye(size, dtype=jnp.bool_)
    entries = jnp.sum(jnp.where(diagonal, inner, 0.0), axis=0)
    inverse = jnp.where(diagonal, 1.0 / entries[None, :], 0.0)
    for sweep in range(NS_ITERS):
        inverse = 2.0 * inverse - product(inverse, product(inner, inverse))
    return inverse


def solve_half(trial_wide, orbitals):
    inner = lax.dot_general(
        trial_wide, orbitals, (((0,), (0,)), ((), ())), precision=lax.Precision.HIGH
    )
    return product(orbitals, newton(inner))


def step_kernel(
    count,
    groups,
    theta_ref,
    chol_ref,
    trial_ref,
    walker_ref,
    fields_ref,
    weight_ref,
    total_ref,
    new_weight_ref,
    chol_v,
    theta_in,
    green,
    spread,
    op_send,
    op_v,
    red,
    part_send,
    part_recv,
    group_send,
    group_recv,
    term_a,
    term_b,
    chol_sem,
    theta_s,
    theta_r,
    part_s,
    part_r,
    group_s,
    group_r,
    op_s,
    op_r,
):
    me = lax.axis_index("pair")
    grp = lax.axis_index("grp")
    vectors, rows, width = chol_v.shape
    span = spread.shape[0] // count
    bits = span.bit_length() - 1
    blocks = rows // span
    offsets = [(count // 2 + s) % count for s in range(count)]
    offsets = [offset for offset in offsets if offset]

    def peer(offset):
        return lax.rem(me + offset, count)

    def group_peer(offset):
        return lax.rem(grp + offset, groups)

    load = pltpu.make_async_copy(chol_ref, chol_v, chol_sem)
    load.start()

    barrier = pltpu.get_barrier_semaphore()
    for offset in offsets:
        pl.semaphore_signal(
            barrier, inc=1, device_id={"pair": peer(offset)}, device_id_type=MESH
        )
    for offset in range(1, groups):
        pl.semaphore_signal(
            barrier, inc=1, device_id={"grp": group_peer(offset)}, device_id_type=MESH
        )
    pl.semaphore_wait(barrier, count - 1 + groups - 1)

    def theta_copy(offset):
        other = peer(offset)
        start = pl.multiple_of(other * rows, rows)
        return pltpu.make_async_remote_copy(
            src_ref=theta_ref.at[pl.ds(start, rows), :],
            dst_ref=theta_in.at[me],
            send_sem=theta_s.at[offset],
            recv_sem=theta_r.at[offset],
            device_id={"pair": other},
            device_id_type=MESH,
        )

    theta_copies = {offset: theta_copy(offset) for offset in offsets}
    for offset in offsets:
        theta_copies[offset].start()

    mine = pl.multiple_of(me * rows, rows)

    def make_green(block):
        return lax.dot_general(
            block, trial_ref[...], NT, preferred_element_type=jnp.float32
        ).astype(jnp.bfloat16)

    green[me] = make_green(theta_ref[pl.ds(mine, rows), :])
    for offset in reversed(offsets):
        theta_copies[offset].wait_recv()
        source = lax.rem(me + count - offset, count)
        green[source] = make_green(theta_in[source])
    load.wait()

    step = min(vectors, 512 // span)
    lines = step * span
    columns = count * span
    line = lax.broadcasted_iota(jnp.int32, (lines, columns), 0)
    column = lax.broadcasted_iota(jnp.int32, (lines, columns), 1)
    same = (line & (span - 1)) == (column & (span - 1))

    def bias_step(i, carry):
        first = pl.multiple_of(i * step, step)
        total = None
        for b in range(blocks):
            held = chol_v[pl.ds(first, step), b * span : (b + 1) * span, :]
            seen = green[:, b * span : (b + 1) * span, :]
            part = lax.dot_general(
                held.reshape(lines, width),
                seen.reshape(columns, width),
                NT,
                preferred_element_type=jnp.float32,
            )
            total = part if total is None else total + part
        kept = jnp.where(same, total, 0.0)
        red[pl.ds(first, step), :] = jnp.sum(kept.reshape(step, span, columns), axis=1)
        return carry

    lax.fori_loop(0, vectors // step, bias_step, 0)

    row = lax.broadcasted_iota(jnp.int32, (count, columns), 0)
    col = lax.broadcasted_iota(jnp.int32, (count, columns), 1)
    owner = (lax.shift_right_logical(col, bits) == row).astype(jnp.float32)
    partial = lax.dot_general(
        owner,
        red[...],
        NT,
        precision=lax.Precision.HIGHEST,
        preferred_element_type=jnp.float32,
    )
    part_send[0:count, :] = partial
    part_send[count : count + 8, :] = weight_ref[...]

    def part_copy(offset):
        return pltpu.make_async_remote_copy(
            src_ref=part_send,
            dst_ref=part_recv.at[me],
            send_sem=part_s.at[offset],
            recv_sem=part_r.at[offset],
            device_id={"pair": peer(offset)},
            device_id_type=MESH,
        )

    part_copies = [part_copy(offset) for offset in offsets]
    for copy in part_copies:
        copy.start()
    part_recv[me] = part_send[...]
    for copy in part_copies:
        copy.wait_recv()
    bias = part_recv[0, 0:count, :]
    for source in range(1, count):
        bias = bias + part_recv[source, 0:count, :]
    xbar = -root_step * bias
    draws = fields_ref[...]
    shifted = (draws - xbar).astype(jnp.bfloat16)

    wide = jnp.broadcast_to(
        shifted.astype(jnp.float32)[:, None, :], (count, span, vectors)
    )
    wide = wide.reshape(columns, vectors).astype(jnp.bfloat16)
    pick_row = lax.broadcasted_iota(jnp.int32, (vectors, lines), 0)
    pick_col = lax.broadcasted_iota(jnp.int32, (vectors, lines), 1)
    pick_col = lax.shift_right_logical(pick_col, bits)
    a_row = lax.broadcasted_iota(jnp.int32, (columns, lines), 0)
    a_col = lax.broadcasted_iota(jnp.int32, (columns, lines), 1)
    a_same = (a_row & (span - 1)) == (a_col & (span - 1))

    def spread_step(i, carry):
        pick = jnp.where(pick_row == pick_col + i * step, 1.0, 0.0).astype(jnp.bfloat16)
        value = jnp.dot(wide, pick, preferred_element_type=jnp.float32)
        start = pl.multiple_of(i * lines, lines)
        spread[:, pl.ds(start, lines)] = jnp.where(a_same, value, 0.0).astype(jnp.bfloat16)
        return carry

    lax.fori_loop(0, vectors // step, spread_step, 0)

    def op_copy(b, offset):
        other = peer(offset)
        start = pl.multiple_of(b * span, span)
        place = pl.multiple_of(me * rows + b * span, span)
        return pltpu.make_async_remote_copy(
            src_ref=op_send.at[other, pl.ds(start, span), :],
            dst_ref=op_v.at[pl.ds(place, span), :],
            send_sem=op_s.at[b, offset],
            recv_sem=op_r.at[b, offset],
            device_id={"pair": other},
            device_id_type=MESH,
        )

    tile = 256

    def op_step(b, carry):
        start = pl.multiple_of(b * span, span)

        def op_tile(t, inner):
            left = pl.multiple_of(t * tile, tile)
            held = chol_v[:, pl.ds(start, span), pl.ds(left, tile)]
            value = root_step * jnp.dot(
                spread[...],
                held.reshape(vectors * span, tile),
                preferred_element_type=jnp.float32,
            )
            op_send[:, pl.ds(start, span), pl.ds(left, tile)] = value.astype(
                jnp.bfloat16
            ).reshape(count, span, tile)
            return inner

        lax.fori_loop(0, width // tile, op_tile, 0)
        for offset in offsets:
            op_copy(b, offset).start()
        return carry

    lax.fori_loop(0, blocks, op_step, 0)

    power = jnp.sum(draws * xbar - 0.5 * xbar * xbar, axis=1, keepdims=True)
    raw = part_recv[:, count : count + 8, :][:, 0, :] * jnp.exp(power)
    group_send[...] = jnp.broadcast_to(jnp.sum(raw, axis=0, keepdims=True), group_send.shape)

    def group_copy(offset):
        return pltpu.make_async_remote_copy(
            src_ref=group_send,
            dst_ref=group_recv.at[grp],
            send_sem=group_s.at[offset],
            recv_sem=group_r.at[offset],
            device_id={"grp": group_peer(offset)},
            device_id_type=MESH,
        )

    group_copies = [group_copy(offset) for offset in range(1, groups)]
    for copy in group_copies:
        copy.start()
    group_recv[grp] = group_send[...]

    term_a[...] = walker_ref[...].astype(jnp.bfloat16)

    def first_order(source):
        start = pl.multiple_of(source * rows, rows)
        place = pl.ds(start, rows)
        value = jnp.dot(op_v[place, :], term_a[...], preferred_element_type=jnp.float32)
        total_ref[place, :] = walker_ref[place, :] + value
        term_b[place, :] = value.astype(jnp.bfloat16)

    op_v[pl.ds(mine, rows), :] = op_send[me]
    first_order(me)
    for offset in reversed(offsets):
        for b in range(blocks):
            op_copy(b, offset).wait_recv()
        first_order(lax.rem(me + count - offset, count))

    held, made = term_b, term_a
    chunk = 256
    for order in range(2, TAYLOR + 1):

        def order_step(i, carry, held=held, made=made, order=order):
            place = pl.ds(pl.multiple_of(i * chunk, chunk), chunk)
            value = jnp.dot(
                op_v[place, :], held[...], preferred_element_type=jnp.float32
            ) / float(order)
            total_ref[place, :] = total_ref[place, :] + value
            if order < TAYLOR:
                made[place, :] = value.astype(jnp.bfloat16)
            return carry

        lax.fori_loop(0, width // chunk, order_step, 0)
        held, made = made, held

    for copy in group_copies:
        copy.wait_recv()
    whole = group_recv[0]
    for source in range(1, groups):
        whole = whole + group_recv[source]
    spot = lax.broadcasted_iota(jnp.int32, raw.shape, 0)
    own = jnp.sum(jnp.where(spot == me, raw, 0.0), axis=0, keepdims=True)
    new_weight_ref[...] = own * (float(count * groups) / whole)

    for offset in offsets:
        theta_copies[offset].wait_send()
    for copy in part_copies + group_copies:
        copy.wait_send()
    for offset in offsets:
        for b in range(blocks):
            op_copy(b, offset).wait_send()


def propagate(theta, chol, trial, walker, fields, weights):
    vectors, rows, width = chol.shape
    occupied = trial.shape[1]
    count = lax.axis_size("pair")
    groups = lax.axis_size("grp")
    span = min(rows, max(16, 256 // count))
    blocks = rows // span
    vmem = pl.BlockSpec(memory_space=pltpu.VMEM)
    dma = pltpu.SemaphoreType.DMA
    return pl.pallas_call(
        functools.partial(step_kernel, count, groups),
        out_shape=(
            jax.ShapeDtypeStruct((width, occupied), jnp.float32),
            jax.ShapeDtypeStruct((8, 128), jnp.float32),
        ),
        in_specs=[vmem, pl.BlockSpec(memory_space=pl.ANY), vmem, vmem, vmem, vmem],
        out_specs=(vmem, vmem),
        scratch_shapes=[
            pltpu.VMEM((vectors, rows, width), jnp.bfloat16),
            pltpu.VMEM((count, rows, occupied), jnp.bfloat16),
            pltpu.VMEM((count, rows, width), jnp.bfloat16),
            pltpu.VMEM((count * span, vectors * span), jnp.bfloat16),
            pltpu.VMEM((count, rows, width), jnp.bfloat16),
            pltpu.VMEM((width, width), jnp.bfloat16),
            pltpu.VMEM((vectors, count * span), jnp.float32),
            pltpu.VMEM((count + 8, vectors), jnp.float32),
            pltpu.VMEM((count, count + 8, vectors), jnp.float32),
            pltpu.VMEM((8, 128), jnp.float32),
            pltpu.VMEM((groups, 8, 128), jnp.float32),
            pltpu.VMEM((width, occupied), jnp.bfloat16),
            pltpu.VMEM((width, occupied), jnp.bfloat16),
            dma,
            dma((count,)),
            dma((count,)),
            dma((count,)),
            dma((count,)),
            dma((groups,)),
            dma((groups,)),
            dma((blocks, count)),
            dma((blocks, count)),
        ],
        compiler_params=pltpu.CompilerParams(
            collective_id=0,
            has_side_effects=True,
            vmem_limit_bytes=60 * 1024 * 1024,
        ),
    )(theta, chol, trial, walker, fields, jnp.broadcast_to(weights[:, None], (8, 128)))


def per_device(chol, trial, walkers, fields, weights):
    trial_wide = trial.astype(jnp.float32)
    walker = walkers[0]
    theta = solve_half(trial_wide, walker).astype(jnp.bfloat16)
    total, spread_weight = propagate(theta, chol, trial, walker, fields, weights)
    half_green = solve_half(trial_wide, total)
    return (total[None], half_green[None], spread_weight[0, 0:1])


def solution(mesh):
    placed = (
        P(None, "pair", None),
        P(),
        P(("grp", "pair"), None, None),
        P("grp", None),
        P(("grp", "pair")),
    )
    return jax.shard_map(
        per_device,
        mesh=mesh,
        in_specs=placed,
        out_specs=(
            P(("grp", "pair"), None, None),
            P(("grp", "pair"), None, None),
            P(("grp", "pair")),
        ),
        check_vma=False,
    )
```

```python
import functools

import jax
import jax.numpy as jnp
from jax import lax
from jax.experimental import pallas as pl
from jax.experimental.pallas import tpu as pltpu
from jax.sharding import PartitionSpec as P

TAYLOR = 4
NS_ITERS = 3

root_step = 0.07

NT = (((1,), (1,)), ((), ()))
TN = (((0,), (0,)), ((), ()))
MESH = pl.DeviceIdType.MESH


def product(left, right):
    return jnp.dot(left, right, precision=lax.Precision.HIGH)


def newton(inner):
    size = inner.shape[-1]
    diagonal = jnp.eye(size, dtype=jnp.bool_)
    entries = jnp.sum(jnp.where(diagonal, inner, 0.0), axis=0)
    scale = 1.0 / entries
    first = scale[:, None] * (inner * scale[None, :])
    inverse = jnp.where(diagonal, 2.0 * scale[None, :], 0.0) - first
    for sweep in range(1, NS_ITERS):
        inverse = 2.0 * inverse - product(inverse, product(inner, inverse))
    return inverse


def halves(value):
    high = value.astype(jnp.bfloat16)
    return high, (value - high.astype(jnp.float32)).astype(jnp.bfloat16)


def step_kernel(
    count,
    groups,
    inverse_ref,
    chol_ref,
    trial_ref,
    walker_ref,
    fields_ref,
    weight_ref,
    total_ref,
    inner_ref,
    new_weight_ref,
    chol_v,
    inverse_high,
    inverse_low,
    theta_out,
    theta_in,
    green,
    spread,
    op_send,
    op_v,
    red,
    part_send,
    part_recv,
    group_send,
    group_recv,
    term_a,
    term_b,
    chol_sem,
    theta_s,
    theta_r,
    part_s,
    part_r,
    group_s,
    group_r,
    op_s,
    op_r,
):
    me = lax.axis_index("pair")
    grp = lax.axis_index("grp")
    vectors, rows, width = chol_v.shape
    span = spread.shape[0] // count
    bits = span.bit_length() - 1
    blocks = rows // span
    offsets = list(range(count - 1, 0, -1))

    def peer(offset):
        other = me
        weight = 1
        while weight < count:
            if offset // weight % 2:
                other = other + weight * (1 - 2 * lax.rem(lax.div(me, weight), 2))
            weight = 2 * weight
        return other

    def group_peer(offset):
        return lax.rem(grp + offset, groups)

    def load(b):
        place = pl.ds(pl.multiple_of(b * span, span), span)
        return pltpu.make_async_copy(
            chol_ref.at[:, place, :], chol_v.at[:, place, :], chol_sem.at[b]
        )

    for b in range(blocks):
        load(b).start()

    barrier = pltpu.get_barrier_semaphore()
    for offset in offsets:
        pl.semaphore_signal(
            barrier, inc=1, device_id={"pair": peer(offset)}, device_id_type=MESH
        )
    for offset in range(1, groups):
        pl.semaphore_signal(
            barrier, inc=1, device_id={"grp": group_peer(offset)}, device_id_type=MESH
        )
    inverse_high[...], inverse_low[...] = halves(inverse_ref[...])
    pl.semaphore_wait(barrier, count - 1 + groups - 1)

    def theta_copy(b, offset):
        other = peer(offset)
        place = pl.ds(pl.multiple_of(b * span, span), span)
        return pltpu.make_async_remote_copy(
            src_ref=theta_out.at[other, place, :],
            dst_ref=theta_in.at[me, place, :],
            send_sem=theta_s.at[b, offset],
            recv_sem=theta_r.at[b, offset],
            device_id={"pair": other},
            device_id_type=MESH,
        )

    occupied = theta_out.shape[2]

    def theta_block(b, carry):
        place = pl.ds(pl.multiple_of(b * span, span), span)
        high, low = halves(walker_ref[:, place, :].reshape(count * span, occupied))
        value = jnp.dot(high, inverse_low[...], preferred_element_type=jnp.float32)
        value = value + jnp.dot(low, inverse_high[...], preferred_element_type=jnp.float32)
        value = value + jnp.dot(high, inverse_high[...], preferred_element_type=jnp.float32)
        theta_out[:, place, :] = value.astype(jnp.bfloat16).reshape(count, span, occupied)
        for offset in offsets:
            theta_copy(b, offset).start()
        return carry

    lax.fori_loop(0, blocks, theta_block, 0)
    theta_in[me] = theta_out[me]

    step = min(vectors, 512 // span)
    lines = step * span
    columns = count * span
    line = lax.broadcasted_iota(jnp.int32, (lines, columns), 0)
    column = lax.broadcasted_iota(jnp.int32, (lines, columns), 1)
    same = (line & (span - 1)) == (column & (span - 1))
    red[...] = jnp.zeros_like(red)

    def bias_block(b, carry):
        for offset in offsets:
            theta_copy(b, offset).wait_recv()
        start = pl.multiple_of(b * span, span)
        green[...] = lax.dot_general(
            trial_ref[...],
            theta_in[:, pl.ds(start, span), :].reshape(columns, occupied),
            NT,
            preferred_element_type=jnp.float32,
        ).astype(jnp.bfloat16)
        load(b).wait()

        def bias_step(i, inner):
            first = pl.multiple_of(i * step, step)
            held = chol_v[pl.ds(first, step), pl.ds(start, span), :]
            part = jnp.dot(
                held.reshape(lines, width), green[...], preferred_element_type=jnp.float32
            )
            kept = jnp.where(same, part, 0.0).reshape(step, span, columns)
            red[pl.ds(first, step), :] = red[pl.ds(first, step), :] + jnp.sum(kept, axis=1)
            return inner

        lax.fori_loop(0, vectors // step, bias_step, 0)
        return carry

    lax.fori_loop(0, blocks, bias_block, 0)

    row = lax.broadcasted_iota(jnp.int32, (count, columns), 0)
    col = lax.broadcasted_iota(jnp.int32, (count, columns), 1)
    owner = (lax.shift_right_logical(col, bits) == row).astype(jnp.float32)
    partial = lax.dot_general(
        owner,
        red[...],
        NT,
        precision=lax.Precision.HIGHEST,
        preferred_element_type=jnp.float32,
    )
    part_send[0:count, :] = partial
    part_send[count : count + 8, :] = weight_ref[...]

    def part_copy(offset):
        return pltpu.make_async_remote_copy(
            src_ref=part_send,
            dst_ref=part_recv.at[me],
            send_sem=part_s.at[offset],
            recv_sem=part_r.at[offset],
            device_id={"pair": peer(offset)},
            device_id_type=MESH,
        )

    part_copies = [part_copy(offset) for offset in offsets]
    for copy in part_copies:
        copy.start()
    part_recv[me] = part_send[...]
    for copy in part_copies:
        copy.wait_recv()
    bias = part_recv[0, 0:count, :]
    for source in range(1, count):
        bias = bias + part_recv[source, 0:count, :]
    xbar = -root_step * bias
    draws = fields_ref[...]
    shifted = (draws - xbar).astype(jnp.bfloat16)

    wide = jnp.broadcast_to(
        shifted.astype(jnp.float32)[:, None, :], (count, span, vectors)
    )
    wide = wide.reshape(columns, vectors).astype(jnp.bfloat16)
    pick_row = lax.broadcasted_iota(jnp.int32, (vectors, lines), 0)
    pick_col = lax.broadcasted_iota(jnp.int32, (vectors, lines), 1)
    pick_col = lax.shift_right_logical(pick_col, bits)
    a_row = lax.broadcasted_iota(jnp.int32, (columns, lines), 0)
    a_col = lax.broadcasted_iota(jnp.int32, (columns, lines), 1)
    a_same = (a_row & (span - 1)) == (a_col & (span - 1))

    def spread_step(i, carry):
        pick = jnp.where(pick_row == pick_col + i * step, 1.0, 0.0).astype(jnp.bfloat16)
        value = jnp.dot(wide, pick, preferred_element_type=jnp.float32)
        start = pl.multiple_of(i * lines, lines)
        spread[:, pl.ds(start, lines)] = jnp.where(a_same, value, 0.0).astype(jnp.bfloat16)
        return carry

    lax.fori_loop(0, vectors // step, spread_step, 0)

    def op_copy(b, offset):
        other = peer(offset)
        place = pl.ds(pl.multiple_of(b * span, span), span)
        return pltpu.make_async_remote_copy(
            src_ref=op_send.at[other, place, :],
            dst_ref=op_v.at[me, place, :],
            send_sem=op_s.at[b, offset],
            recv_sem=op_r.at[b, offset],
            device_id={"pair": other},
            device_id_type=MESH,
        )

    tile = 256

    def op_step(b, carry):
        start = pl.multiple_of(b * span, span)

        def op_tile(t, inner):
            left = pl.multiple_of(t * tile, tile)
            held = chol_v[:, pl.ds(start, span), pl.ds(left, tile)]
            value = root_step * jnp.dot(
                spread[...],
                held.reshape(vectors * span, tile),
                preferred_element_type=jnp.float32,
            )
            op_send[:, pl.ds(start, span), pl.ds(left, tile)] = value.astype(
                jnp.bfloat16
            ).reshape(count, span, tile)
            return inner

        lax.fori_loop(0, width // tile, op_tile, 0)
        for offset in offsets:
            op_copy(b, offset).start()
        return carry

    lax.fori_loop(0, blocks, op_step, 0)

    power = jnp.sum(draws * xbar - 0.5 * xbar * xbar, axis=1, keepdims=True)
    raw = part_recv[:, count : count + 8, :][:, 0, :] * jnp.exp(power)
    group_send[...] = jnp.broadcast_to(jnp.sum(raw, axis=0, keepdims=True), group_send.shape)

    def group_copy(offset):
        return pltpu.make_async_remote_copy(
            src_ref=group_send,
            dst_ref=group_recv.at[grp],
            send_sem=group_s.at[offset],
            recv_sem=group_r.at[offset],
            device_id={"grp": group_peer(offset)},
            device_id_type=MESH,
        )

    group_copies = [group_copy(offset) for offset in range(1, groups)]
    for copy in group_copies:
        copy.start()
    group_recv[grp] = group_send[...]

    term_a[...] = walker_ref[...].reshape(width, occupied).astype(jnp.bfloat16)

    op_v[me] = op_send[me]

    def first_order(b, carry):
        for offset in offsets:
            op_copy(b, offset).wait_recv()
        place = pl.ds(pl.multiple_of(b * span, span), span)
        value = jnp.dot(
            op_v[:, place, :].reshape(columns, width),
            term_a[...],
            preferred_element_type=jnp.float32,
        ).reshape(count, span, occupied)
        total_ref[:, place, :] = walker_ref[:, place, :] + value
        term_b[:, place, :] = value.astype(jnp.bfloat16)
        return carry

    lax.fori_loop(0, blocks, first_order, 0)

    group_rows = max(1, 256 // rows)
    chunk = group_rows * rows
    seen, made = term_b, term_a
    inner_ref[...] = jnp.zeros_like(inner_ref)
    for order in range(2, TAYLOR + 1):

        def order_step(i, carry, seen=seen, made=made, order=order):
            place = pl.ds(i * group_rows, group_rows)
            value = jnp.dot(
                op_v[place].reshape(chunk, width),
                seen[...].reshape(width, occupied),
                preferred_element_type=jnp.float32,
            ) / float(order)
            total = total_ref[place].reshape(chunk, occupied) + value
            total_ref[place] = total.reshape(group_rows, rows, occupied)
            if order == TAYLOR:
                bra = trial_ref[pl.ds(pl.multiple_of(i * chunk, chunk), chunk), :]
                high, low = halves(total)
                added = lax.dot_general(bra, low, TN, preferred_element_type=jnp.float32)
                added = added + lax.dot_general(bra, high, TN, preferred_element_type=jnp.float32)
                inner_ref[...] = inner_ref[...] + added
            else:
                if made is term_a:
                    made[pl.ds(pl.multiple_of(i * chunk, chunk), chunk), :] = value.astype(jnp.bfloat16)
                else:
                    made[place] = value.astype(jnp.bfloat16).reshape(group_rows, rows, occupied)
            return carry

        lax.fori_loop(0, count // group_rows, order_step, 0)
        seen, made = made, seen

    for copy in group_copies:
        copy.wait_recv()
    whole = group_recv[0]
    for source in range(1, groups):
        whole = whole + group_recv[source]
    spot = lax.broadcasted_iota(jnp.int32, raw.shape, 0)
    own = jnp.sum(jnp.where(spot == me, raw, 0.0), axis=0, keepdims=True)
    new_weight_ref[...] = own * (float(count * groups) / whole)

    for copy in part_copies + group_copies:
        copy.wait_send()
    for offset in offsets:
        for b in range(blocks):
            theta_copy(b, offset).wait_send()
            op_copy(b, offset).wait_send()


def propagate(inverse, chol, trial, walker, fields, weights):
    vectors, rows, width = chol.shape
    occupied = trial.shape[1]
    count = lax.axis_size("pair")
    groups = lax.axis_size("grp")
    span = min(rows, max(16, 256 // count))
    blocks = rows // span
    vmem = pl.BlockSpec(memory_space=pltpu.VMEM)
    dma = pltpu.SemaphoreType.DMA
    return pl.pallas_call(
        functools.partial(step_kernel, count, groups),
        out_shape=(
            jax.ShapeDtypeStruct((count, rows, occupied), jnp.float32),
            jax.ShapeDtypeStruct((occupied, occupied), jnp.float32),
            jax.ShapeDtypeStruct((8, 128), jnp.float32),
        ),
        in_specs=[vmem, pl.BlockSpec(memory_space=pl.ANY), vmem, vmem, vmem, vmem],
        out_specs=(vmem, vmem, vmem),
        scratch_shapes=[
            pltpu.VMEM((vectors, rows, width), jnp.bfloat16),
            pltpu.VMEM((occupied, occupied), jnp.bfloat16),
            pltpu.VMEM((occupied, occupied), jnp.bfloat16),
            pltpu.VMEM((count, rows, occupied), jnp.bfloat16),
            pltpu.VMEM((count, rows, occupied), jnp.bfloat16),
            pltpu.VMEM((width, count * span), jnp.bfloat16),
            pltpu.VMEM((count * span, vectors * span), jnp.bfloat16),
            pltpu.VMEM((count, rows, width), jnp.bfloat16),
            pltpu.VMEM((count, rows, width), jnp.bfloat16),
            pltpu.VMEM((vectors, count * span), jnp.float32),
            pltpu.VMEM((count + 8, vectors), jnp.float32),
            pltpu.VMEM((count, count + 8, vectors), jnp.float32),
            pltpu.VMEM((8, 128), jnp.float32),
            pltpu.VMEM((groups, 8, 128), jnp.float32),
            pltpu.VMEM((width, occupied), jnp.bfloat16),
            pltpu.VMEM((count, rows, occupied), jnp.bfloat16),
            dma((blocks,)),
            dma((blocks, count)),
            dma((blocks, count)),
            dma((count,)),
            dma((count,)),
            dma((groups,)),
            dma((groups,)),
            dma((blocks, count)),
            dma((blocks, count)),
        ],
        compiler_params=pltpu.CompilerParams(
            collective_id=0,
            has_side_effects=True,
            vmem_limit_bytes=60 * 1024 * 1024,
        ),
    )(inverse, chol, trial, walker.reshape(count, rows, occupied), fields, jnp.broadcast_to(weights[:, None], (8, 128)))


def per_device(chol, trial, walkers, fields, weights):
    walker = walkers[0]
    inner = lax.dot_general(
        trial.astype(jnp.float32), walker, TN, precision=lax.Precision.HIGH
    )
    inverse = newton(inner)
    total, inner_next, spread_weight = propagate(inverse, chol, trial, walker, fields, weights)
    total = total.reshape(walker.shape)
    half_green = product(total, newton(inner_next))
    return (total[None], half_green[None], spread_weight[0, 0:1])


def solution(mesh):
    placed = (
        P(None, "pair", None),
        P(),
        P(("grp", "pair"), None, None),
        P("grp", None),
        P(("grp", "pair")),
    )
    return jax.shard_map(
        per_device,
        mesh=mesh,
        in_specs=placed,
        out_specs=(
            P(("grp", "pair"), None, None),
            P(("grp", "pair"), None, None),
            P(("grp", "pair")),
        ),
        check_vma=False,
    )
```
